32 devices in a mesh: gx: 8 (over y, x, core), gy: 4 (over z).
Axes of the slice: x: 2, y: 2, z: 4, core: 2. Of those that a mesh axis runs over, the one named last changes fastest.
Arguments:
- fine: bfloat16 [1024, 8, 256, 128], P(('gx', 'gy')), may hold values from -1500 to 1500
- patch_count: int32 [32], P(('gx', 'gy')), may hold values from 0 to 32, as said below
- block_place: int32 [32, 16], P(('gx', 'gy')), may hold values from 0 to 15, each once within a row
Outputs:
- factor: float32 [128, 128], replicated
- modes: bfloat16 [131072, 128], P(('gx', 'gy'))
The draws below stay inside these ranges and needn't reach their ends.
Inputs may be any that keep to these rules, and one draw needn't show every extreme that they name: `patch_count`: devices 2k and 2k + 1 in the numbering d = (index along gx) * 4 + (index along gy) hold 32 patches together; in every draw some even device holds 32 and some odd device holds 32.
All inputs are finite; a program needn't handle non-finite values.
Results may differ from the reference program's by a relative error of at most 0.004.
The reference program's roundings to bfloat16 on the way (of `coarse_slot` and `coarse`) count: a program that leaves them out, or rounds other values in their place, can miss the bound.
Values may be sent and summed in bfloat16 or wider, within the bound.
A program may use at most 64 MiB of HBM per device.

```python
import math
import jax
import jax.numpy as jnp
from jax import lax

S = 128
PATCH = 256
CB = 16
PAIRS = 16
SLOTS_ALL = 1024
ROWS = 131072
N_GX = 8
N_GY = 4


def draw_fine(key, part):
    keys = jax.random.split(jax.random.fold_in(key, 11), 3)
    shape = (SLOTS_ALL, 8, PATCH, S)
    noise = jnp.clip(jax.random.normal(keys[0], shape, jnp.float32), -6.0, 6.0)
    column = jnp.exp(jax.random.uniform(keys[1], (S,), jnp.float32, 0.0, math.log(10.0)))
    cell = jnp.exp(jax.random.uniform(keys[2], (SLOTS_ALL, 1, PATCH, 1), jnp.float32, math.log(0.5), math.log(5.0)))
    device_pos = (jnp.arange(SLOTS_ALL) // (2 * CB)).astype(jnp.float32)
    device_scale = 1.0 + 2.0 * device_pos / (2 * PAIRS - 1)
    values = noise * column * cell * device_scale[:, None, None, None]
    return values.astype(jnp.bfloat16)


def draw_patch_count(key, part):
    keys = jax.random.split(jax.random.fold_in(key, 7), 3)
    excess = jax.random.randint(keys[0], (PAIRS,), -CB, CB + 1)
    first_pair = jax.random.randint(keys[1], (), 0, PAIRS)
    second_pair = (first_pair + 1 + jax.random.randint(keys[2], (), 0, PAIRS - 1)) % PAIRS
    excess = excess.at[first_pair].set(CB).at[second_pair].set(-CB)
    counts = jnp.stack([CB + excess, CB - excess], axis=1).reshape(2 * PAIRS)
    return counts.astype(jnp.int32)


def setup_inputs(seed: int = 0) -> dict:
    splits = jax.random.split(jax.random.key(seed), 4)
    return {
        "fine": draw_fine(jax.random.fold_in(splits[3], 71), 0),
        "patch_count": draw_patch_count(jax.random.fold_in(splits[3], 71), 0),
        "block_place": jax.vmap(lambda own: jax.random.permutation(own, CB))(jax.random.split(splits[2], (2 * PAIRS))).reshape((2 * PAIRS, CB)).astype(jnp.int32),
    }


def restrict_block(fine_block):
    return (lax.optimization_barrier(jnp.sum(fine_block, axis=1, dtype=jnp.float32)) * 0.125).astype(jnp.bfloat16)

def lower_factor(gram):
    width = gram.shape[0]
    index_col = jnp.arange(width, dtype=jnp.int32)

    def column_step(column, lower):
        partial_col = gram[:, column] - jnp.dot(lower, lower[column], precision=lax.Precision.HIGHEST)
        pivot = jnp.sqrt(partial_col[column])
        values = jnp.where(index_col > column, partial_col / pivot, jnp.where(index_col == column, pivot, 0.0))
        marker = (index_col == column).astype(jnp.float32)
        return lower + values[:, None] * marker[None, :]
    return lax.fori_loop(0, width, column_step, jnp.zeros((width, width), jnp.float32))

def lower_inverse(lower):
    width = lower.shape[0]
    index_col = jnp.arange(width, dtype=jnp.int32)
    identity = jnp.eye(width, dtype=jnp.float32)

    def row_step(row, inverse):
        known = jnp.where(index_col < row, lower[row], 0.0)
        values = (identity[row] - jnp.dot(known, inverse, precision=lax.Precision.HIGHEST)) / lower[row, row]
        marker = (index_col == row).astype(jnp.float32)
        return inverse + marker[:, None] * values[None, :]
    return lax.fori_loop(0, width, row_step, jnp.zeros((width, width), jnp.float32))

def reference(fine, patch_count, block_place):
    device_total = N_GX * N_GY
    slot_width = 2 * CB
    shaped = fine.reshape(device_total, slot_width, 8, PATCH, S)
    coarse_slot = lax.map(restrict_block, shaped).reshape(device_total * slot_width, PATCH, S)
    ends = jnp.cumsum(patch_count).astype(jnp.int32)
    starts = (ends - patch_count).astype(jnp.int32)
    block_ids = jnp.arange(device_total * CB, dtype=jnp.int32)
    holder = lax.optimization_barrier(jnp.sum((ends[None, :] <= block_ids[:, None]).astype(jnp.int32), axis=1)).astype(jnp.int32)
    source = (holder * slot_width + block_ids - starts[holder]).astype(jnp.int32)
    wanted = (jnp.arange(device_total, dtype=jnp.int32)[:, None] * CB + block_place).reshape(-1).astype(jnp.int32)
    coarse = jnp.take(coarse_slot, source[wanted], axis=0).reshape(ROWS, S)
    gram = lax.dot_general(coarse, coarse, (((0,), (0,)), ((), ())), preferred_element_type=jnp.float32) / ROWS
    lower = lower_factor(gram)
    factor = lower.T
    upper_inv = lower_inverse(lower).T
    modes = jnp.dot(coarse.astype(jnp.float32), upper_inv, precision=lax.Precision.HIGHEST)
    return (factor, modes.astype(jnp.bfloat16))
```

```python
import functools

import jax
import jax.numpy as jnp
from jax import lax
from jax.experimental import pallas as pl
from jax.experimental.pallas import tpu as pltpu
from jax.sharding import PartitionSpec as P

MESH = pl.DeviceIdType.MESH


def average_kernel(meta_ref, fine_ref, avg_ref, gram_ref):
    step = pl.program_id(0)
    slots, children, cells, width = fine_ref.shape

    @pl.when(step == 0)
    def _():
        gram_ref[...] = jnp.zeros_like(gram_ref)

    piece = 32
    for slot in range(slots):
        valid = meta_ref[0] * meta_ref[2] + step * slots + slot < meta_ref[1]
        for row in range(0, cells, piece):
            rows = pl.ds(row, piece)
            total = fine_ref[slot, 0, rows, :].astype(jnp.float32)
            for child in range(1, children):
                total += fine_ref[slot, child, rows, :].astype(jnp.float32)
            avg_ref[slot, rows, :] = (total * (1.0 / children)).astype(jnp.bfloat16)
        weight = jnp.where(valid, 1.0, 0.0).astype(jnp.float32)
        part = avg_ref[slot]
        gram_ref[...] += weight * lax.dot_general(
            part, part, (((0,), (0,)), ((), ())), preferred_element_type=jnp.float32
        )


def average_half(fine, half, count):
    slot_total, children, cells, width = fine.shape
    blocks = slot_total // 2
    slots = 2 if blocks % 2 == 0 else 1
    steps = blocks // slots
    meta = jnp.stack([half, count, jnp.int32(blocks)])
    return pl.pallas_call(
        average_kernel,
        grid_spec=pltpu.PrefetchScalarGridSpec(
            num_scalar_prefetch=1,
            grid=(steps,),
            in_specs=[
                pl.BlockSpec(
                    (slots, children, cells, width),
                    lambda i, meta: (meta[0] * steps + i, 0, 0, 0),
                )
            ],
            out_specs=[
                pl.BlockSpec((slots, cells, width), lambda i, meta: (i, 0, 0)),
                pl.BlockSpec((width, width), lambda i, meta: (0, 0)),
            ],
        ),
        out_shape=[
            jax.ShapeDtypeStruct((blocks, cells, width), jnp.bfloat16),
            jax.ShapeDtypeStruct((width, width), jnp.float32),
        ],
        compiler_params=pltpu.CompilerParams(vmem_limit_bytes=56 * 2**20),
        cost_estimate=pl.CostEstimate(
            flops=2 * blocks * cells * width * width,
            bytes_accessed=fine.size + fine.size // children,
            transcendentals=0,
        ),
    )(meta, fine)


def sum_kernel(n_gx, n_gy, row_total, first_ref, second_ref, out_ref, local, parts, planes, send, recv):
    gx, gy = lax.axis_index("gx"), lax.axis_index("gy")
    width = out_ref.shape[0]
    rows = width // n_gx
    barrier = pltpu.get_barrier_semaphore()
    for apart in range(1, n_gx):
        pl.semaphore_signal(
            barrier, inc=1, device_id=(lax.rem(gx + apart, n_gx), gy), device_id_type=MESH
        )
    for apart in range(1, n_gy):
        pl.semaphore_signal(
            barrier, inc=1, device_id=(gx, lax.rem(gy + apart, n_gy)), device_id_type=MESH
        )
    local[...] = first_ref[...] + second_ref[...]
    pl.semaphore_wait(barrier, n_gx + n_gy - 2)

    copies = []
    for apart in range(1, n_gx):
        there = lax.rem(gx + apart, n_gx)
        copy = pltpu.make_async_remote_copy(
            src_ref=local.at[pl.ds(pl.multiple_of(there * rows, rows), rows)],
            dst_ref=parts.at[apart],
            send_sem=send.at[0, apart],
            recv_sem=recv.at[0, apart],
            device_id=(there, gy),
            device_id_type=MESH,
        )
        copy.start()
        copies.append(copy)
    total = local[pl.ds(pl.multiple_of(gx * rows, rows), rows), :]
    for apart in range(1, n_gx):
        copies[apart - 1].wait_recv()
        total += parts[apart]
    planes[gy] = total

    for apart in range(1, n_gy):
        copy = pltpu.make_async_remote_copy(
            src_ref=planes.at[gy],
            dst_ref=planes.at[gy],
            send_sem=send.at[1, apart],
            recv_sem=recv.at[1, apart],
            device_id=(gx, lax.rem(gy + apart, n_gy)),
            device_id_type=MESH,
        )
        copy.start()
        copies.append(copy)
    for apart in range(1, n_gy):
        copies[n_gx - 2 + apart].wait_recv()
    total = planes[0]
    for plane in range(1, n_gy):
        total += planes[plane]
    mine = pl.ds(pl.multiple_of(gx * rows, rows), rows)
    out_ref[mine, :] = total / row_total

    last = []
    for apart in range(1, n_gx):
        copy = pltpu.make_async_remote_copy(
            src_ref=out_ref.at[mine],
            dst_ref=out_ref.at[mine],
            send_sem=send.at[2, apart],
            recv_sem=recv.at[2, apart],
            device_id=(lax.rem(gx + apart, n_gx), gy),
            device_id_type=MESH,
        )
        copy.start()
        last.append(copy)
    for copy in copies:
        copy.wait_send()
    for copy in last:
        copy.wait()


def sum_everywhere(first, second, row_total):
    n_gx, n_gy = lax.axis_size("gx"), lax.axis_size("gy")
    width = first.shape[0]
    rows = width // n_gx
    most = max(n_gx, n_gy)
    return pl.pallas_call(
        functools.partial(sum_kernel, n_gx, n_gy, row_total),
        out_shape=jax.ShapeDtypeStruct((width, width), jnp.float32),
        in_specs=[pl.BlockSpec(memory_space=pltpu.VMEM)] * 2,
        out_specs=pl.BlockSpec(memory_space=pltpu.VMEM),
        scratch_shapes=[
            pltpu.VMEM((width, width), jnp.float32),
            pltpu.VMEM((n_gx, rows, width), jnp.float32),
            pltpu.VMEM((n_gy, rows, width), jnp.float32),
            pltpu.SemaphoreType.DMA((3, most)),
            pltpu.SemaphoreType.DMA((3, most)),
        ],
        compiler_params=pltpu.CompilerParams(collective_id=0, has_side_effects=True),
        cost_estimate=pl.CostEstimate(flops=0, bytes_accessed=32 * 2**20, transcendentals=0),
    )(first, second)


def factor_kernel(gram_ref, factor_ref, split_ref):
    width = gram_ref.shape[0]
    step = 8
    groups = width // step
    lane = lax.broadcasted_iota(jnp.int32, (step, width), 1)
    sub = lax.broadcasted_iota(jnp.int32, (step, width), 0)
    gram = [gram_ref[g * step : (g + 1) * step, :] for g in range(groups)]
    inv = [(lane == sub + g * step).astype(jnp.float32) for g in range(groups)]
    done = []
    for g in range(groups):
        base = g * step
        cols = [
            [jnp.broadcast_to(gram[h][:, base + j : base + j + 1], (step, width)) for h in range(g, groups)]
            for j in range(step)
        ]
        rows = [jnp.broadcast_to(gram[g][j : j + 1, :], (step, width)) for j in range(step)]
        irows = [jnp.broadcast_to(inv[g][j : j + 1, :], (step, width)) for j in range(step)]
        scaled = []
        upper = jnp.zeros((step, width), jnp.float32)
        lower = jnp.zeros((step, width), jnp.float32)
        for j in range(step):
            splat = [jnp.broadcast_to(cols[j][0][i : i + 1, :], (step, width)) for i in range(j, step)]
            pivot = splat[0]
            over = 1.0 / pivot
            srow, sirow = rows[j] * over, irows[j] * over
            scaled.append((srow, sirow))
            for i in range(j + 1, step):
                ratio = splat[i - j] * over
                rows[i] = rows[i] - splat[i - j] * srow
                irows[i] = irows[i] - splat[i - j] * sirow
                cols[i] = [cols[i][h] - ratio * cols[j][h] for h in range(groups - g)]
            root = lax.rsqrt(pivot)
            upper = jnp.where(sub == j, rows[j] * root, upper)
            lower = jnp.where(sub == j, irows[j] * root, lower)
        factor_ref[base : base + step, :] = jnp.where(lane >= sub + base, upper, 0.0)
        done.append(lower)
        for h in range(g + 1, groups):
            for j in range(step):
                gram[h] = gram[h] - cols[j][h - g] * scaled[j][0]
                inv[h] = inv[h] - cols[j][h - g] * scaled[j][1]
    whole = jnp.concatenate(done, axis=0).T
    high = whole.astype(jnp.bfloat16)
    split_ref[:, :width] = high
    split_ref[:, width:] = (whole - high.astype(jnp.float32)).astype(jnp.bfloat16)


def factor_and_inverse(gram):
    width = gram.shape[0]
    return pl.pallas_call(
        factor_kernel,
        out_shape=[
            jax.ShapeDtypeStruct((width, width), jnp.float32),
            jax.ShapeDtypeStruct((width, 2 * width), jnp.bfloat16),
        ],
        in_specs=[pl.BlockSpec(memory_space=pltpu.VMEM)],
        out_specs=[pl.BlockSpec(memory_space=pltpu.VMEM)] * 2,
        compiler_params=pltpu.CompilerParams(vmem_limit_bytes=32 * 2**20),
        cost_estimate=pl.CostEstimate(flops=0, bytes_accessed=32 * 2**20, transcendentals=0),
    )(gram)


def modes_kernel(which_ref, place_ref, split_ref, kept_ref, sent_ref, moved_ref, out_ref, rows, result, in_sem, out_sem):
    blocks, cells, width = rows.shape
    sources = (kept_ref, sent_ref, moved_ref)
    for block in range(blocks):
        for index, source in enumerate(sources):

            @pl.when(which_ref[block] == index)
            def _():
                pltpu.make_async_copy(
                    source.at[place_ref[block]], rows.at[block], in_sem.at[block]
                ).start()

    split = split_ref[...]
    copies = []
    for block in range(blocks):
        pltpu.make_async_copy(kept_ref.at[0], rows.at[block], in_sem.at[block]).wait()
        both = jnp.dot(rows[block], split, preferred_element_type=jnp.float32)
        result[block] = (both[:, :width] + both[:, width:]).astype(jnp.bfloat16)
        copy = pltpu.make_async_copy(
            result.at[block], out_ref.at[pl.ds(block * cells, cells)], out_sem.at[block]
        )
        copy.start()
        copies.append(copy)
    for copy in copies:
        copy.wait()


def make_modes(which, place, split, kept, sent, moved):
    blocks, cells, width = kept.shape
    any_spec = pl.BlockSpec(memory_space=pl.ANY)
    smem = pl.BlockSpec(memory_space=pltpu.SMEM)
    return pl.pallas_call(
        modes_kernel,
        out_shape=jax.ShapeDtypeStruct((blocks * cells, width), jnp.bfloat16),
        in_specs=[smem, smem, pl.BlockSpec(memory_space=pltpu.VMEM), any_spec, any_spec, any_spec],
        out_specs=any_spec,
        scratch_shapes=[
            pltpu.VMEM((blocks, cells, width), jnp.bfloat16),
            pltpu.VMEM((blocks, cells, width), jnp.bfloat16),
            pltpu.SemaphoreType.DMA((blocks,)),
            pltpu.SemaphoreType.DMA((blocks,)),
        ],
        compiler_params=pltpu.CompilerParams(vmem_limit_bytes=32 * 2**20),
        cost_estimate=pl.CostEstimate(
            flops=4 * blocks * cells * width * width,
            bytes_accessed=4 * blocks * cells * width,
            transcendentals=0,
        ),
    )(which, place, split, kept, sent, moved)


def shards(fine, patch_count, block_place):
    slot_total = fine.shape[0]
    blocks = slot_total // 2
    patch_cells = fine.shape[2]
    parity = lax.axis_index("gy") % 2
    held_count = patch_count[0]
    send_half = 1 - parity
    sent, sent_gram = average_half(fine, send_half, held_count)
    pairs = [(source, source ^ 1) for source in range(lax.axis_size("gy"))]
    moved = lax.ppermute(sent, "gy", pairs)
    kept, kept_gram = average_half(fine, parity, held_count)
    row_total = blocks * patch_cells * lax.axis_size("gx") * lax.axis_size("gy")
    gram = sum_everywhere(sent_gram, kept_gram, row_total)
    factor, split = factor_and_inverse(gram)

    excess = jnp.where(parity == 0, held_count - blocks, blocks - held_count)
    wanted = block_place[0]
    is_moved = jnp.where(parity == 0, wanted >= blocks + excess, wanted < excess)
    own = jnp.where(parity == 0, wanted, wanted - excess)
    is_sent = own // blocks == send_half
    which = jnp.where(is_moved, 2, jnp.where(is_sent, 1, 0)).astype(jnp.int32)
    moved_place = jnp.where(parity == 0, wanted - blocks - excess, wanted)
    place = jnp.where(is_moved, moved_place, own % blocks)
    place = jnp.clip(place, 0, blocks - 1).astype(jnp.int32)
    modes = make_modes(which, place, split, kept, sent, moved)
    return (factor, modes)


def solution(mesh):
    return jax.shard_map(
        shards,
        mesh=mesh,
        in_specs=(P(("gx", "gy"), None, None, None), P(("gx", "gy")), P(("gx", "gy"), None)),
        out_specs=(P(), P(("gx", "gy"), None)),
        check_vma=False,
    )
```

```python
import functools

import jax
import jax.numpy as jnp
from jax import lax
from jax.experimental import pallas as pl
from jax.experimental.pallas import tpu as pltpu
from jax.sharding import PartitionSpec as P

MESH = pl.DeviceIdType.MESH


def average_kernel(lens, meta_ref, fine_ref, *refs):
    step = pl.program_id(0)
    slots, children, cells, width = fine_ref.shape
    outs, gram_ref, masked = refs[: len(lens)], refs[-2], refs[-1]

    @pl.when(step == 0)
    def _():
        gram_ref[...] = jnp.zeros_like(gram_ref)

    def work(avg_ref):
        piece = 32
        acc = None
        for slot in range(slots):
            number = lax.rem(meta_ref[0] + step * slots + slot, meta_ref[2])
            weight = jnp.where(number < meta_ref[1], 1.0, 0.0).astype(jnp.float32)
            for row in range(0, cells, piece):
                rows = pl.ds(row, piece)
                total = fine_ref[slot, 0, rows, :].astype(jnp.float32)
                for child in range(1, children):
                    total += fine_ref[slot, child, rows, :].astype(jnp.float32)
                mean = total * (1.0 / children)
                avg_ref[slot, rows, :] = mean.astype(jnp.bfloat16)
                masked[slot, rows, :] = (mean * weight).astype(jnp.bfloat16)
            part = masked[slot]
            term = lax.dot_general(
                part, part, (((0,), (0,)), ((), ())), preferred_element_type=jnp.float32
            )
            acc = term if acc is None else acc + term
        gram_ref[...] += acc

    start = 0
    for length, out in zip(lens, outs):
        if len(lens) == 1:
            work(out)
        else:
            pl.when((step >= start) & (step < start + length))(functools.partial(work, out))
        start += length


def average_range(fine, first, count, lens):
    slot_total, children, cells, width = fine.shape
    slots = slot_total // 8
    total = sum(lens)
    steps = [length // slots for length in lens]
    starts = [sum(steps[:k]) for k in range(len(steps))]
    meta = jnp.stack([first, count, jnp.int32(slot_total)])

    def out_spec(start, length):
        return pl.BlockSpec(
            (slots, cells, width), lambda i, meta: (jnp.clip(i - start, 0, length - 1), 0, 0)
        )

    return pl.pallas_call(
        functools.partial(average_kernel, steps),
        grid_spec=pltpu.PrefetchScalarGridSpec(
            num_scalar_prefetch=1,
            grid=(sum(steps),),
            in_specs=[
                pl.BlockSpec(
                    (slots, children, cells, width),
                    lambda i, meta: (lax.rem(meta[0] // slots + i, slot_total // slots), 0, 0, 0),
                )
            ],
            out_specs=[out_spec(start, length) for start, length in zip(starts, steps)]
            + [pl.BlockSpec((width, width), lambda i, meta: (0, 0))],
            scratch_shapes=[pltpu.VMEM((slots, cells, width), jnp.bfloat16)],
        ),
        out_shape=[jax.ShapeDtypeStruct((length, cells, width), jnp.bfloat16) for length in lens]
        + [jax.ShapeDtypeStruct((width, width), jnp.float32)],
        compiler_params=pltpu.CompilerParams(vmem_limit_bytes=56 * 2**20),
        cost_estimate=pl.CostEstimate(
            flops=2 * total * cells * width * width,
            bytes_accessed=4 * total * (children + 1) * cells * width,
            transcendentals=0,
        ),
    )(meta, fine)


def sum_kernel(n_gx, n_gy, row_total, first_ref, second_ref, out_ref, local, parts, planes, send, recv):
    gx, gy = lax.axis_index("gx"), lax.axis_index("gy")
    width = out_ref.shape[0]
    rows = width // n_gx
    barrier = pltpu.get_barrier_semaphore()
    for apart in range(1, n_gx):
        pl.semaphore_signal(
            barrier, inc=1, device_id=(lax.rem(gx + apart, n_gx), gy), device_id_type=MESH
        )
    for apart in range(1, n_gy):
        pl.semaphore_signal(
            barrier, inc=1, device_id=(gx, lax.rem(gy + apart, n_gy)), device_id_type=MESH
        )
    local[...] = first_ref[...] + second_ref[...]
    pl.semaphore_wait(barrier, n_gx + n_gy - 2)

    copies = []
    for apart in range(1, n_gx):
        there = lax.rem(gx + apart, n_gx)
        copy = pltpu.make_async_remote_copy(
            src_ref=local.at[pl.ds(pl.multiple_of(there * rows, rows), rows)],
            dst_ref=parts.at[apart],
            send_sem=send.at[0, apart],
            recv_sem=recv.at[0, apart],
            device_id=(there, gy),
            device_id_type=MESH,
        )
        copy.start()
        copies.append(copy)
    total = local[pl.ds(pl.multiple_of(gx * rows, rows), rows), :]
    for apart in range(1, n_gx):
        copies[apart - 1].wait_recv()
        total += parts[apart]
    planes[gy] = total

    for apart in range(1, n_gy):
        copy = pltpu.make_async_remote_copy(
            src_ref=planes.at[gy],
            dst_ref=planes.at[gy],
            send_sem=send.at[1, apart],
            recv_sem=recv.at[1, apart],
            device_id=(gx, lax.rem(gy + apart, n_gy)),
            device_id_type=MESH,
        )
        copy.start()
        copies.append(copy)
    for apart in range(1, n_gy):
        copies[n_gx - 2 + apart].wait_recv()
    total = planes[0]
    for plane in range(1, n_gy):
        total += planes[plane]
    mine = pl.ds(pl.multiple_of(gx * rows, rows), rows)
    out_ref[mine, :] = total / row_total

    last = []
    for apart in range(1, n_gx):
        copy = pltpu.make_async_remote_copy(
            src_ref=out_ref.at[mine],
            dst_ref=out_ref.at[mine],
            send_sem=send.at[2, apart],
            recv_sem=recv.at[2, apart],
            device_id=(lax.rem(gx + apart, n_gx), gy),
            device_id_type=MESH,
        )
        copy.start()
        last.append(copy)
    for copy in copies:
        copy.wait_send()
    for copy in last:
        copy.wait()


def sum_everywhere(first, second, row_total):
    n_gx, n_gy = lax.axis_size("gx"), lax.axis_size("gy")
    width = first.shape[0]
    rows = width // n_gx
    most = max(n_gx, n_gy)
    return pl.pallas_call(
        functools.partial(sum_kernel, n_gx, n_gy, row_total),
        out_shape=jax.ShapeDtypeStruct((width, width), jnp.float32),
        in_specs=[pl.BlockSpec(memory_space=pltpu.VMEM)] * 2,
        out_specs=pl.BlockSpec(memory_space=pltpu.VMEM),
        scratch_shapes=[
            pltpu.VMEM((width, width), jnp.float32),
            pltpu.VMEM((n_gx, rows, width), jnp.float32),
            pltpu.VMEM((n_gy, rows, width), jnp.float32),
            pltpu.SemaphoreType.DMA((3, most)),
            pltpu.SemaphoreType.DMA((3, most)),
        ],
        compiler_params=pltpu.CompilerParams(collective_id=0, has_side_effects=True),
        cost_estimate=pl.CostEstimate(flops=0, bytes_accessed=32 * 2**20, transcendentals=0),
    )(first, second)


def factor_kernel(gram_ref, factor_ref, split_ref):
    width = gram_ref.shape[0]
    step = 8
    groups = width // step
    lane = lax.broadcasted_iota(jnp.int32, (step, width), 1)
    sub = lax.broadcasted_iota(jnp.int32, (step, width), 0)
    gram = [gram_ref[g * step : (g + 1) * step, :] for g in range(groups)]
    inv = [(lane == sub + g * step).astype(jnp.float32) for g in range(groups)]
    done = []
    for g in range(groups):
        base = g * step
        cols = [
            [jnp.broadcast_to(gram[h][:, base + j : base + j + 1], (step, width)) for h in range(g, groups)]
            for j in range(step)
        ]
        rows = [jnp.broadcast_to(gram[g][j : j + 1, :], (step, width)) for j in range(step)]
        irows = [jnp.broadcast_to(inv[g][j : j + 1, :], (step, width)) for j in range(step)]
        scaled = []
        upper = jnp.zeros((step, width), jnp.float32)
        lower = jnp.zeros((step, width), jnp.float32)
        for j in range(step):
            splat = [jnp.broadcast_to(cols[j][0][i : i + 1, :], (step, width)) for i in range(j, step)]
            pivot = splat[0]
            over = 1.0 / pivot
            srow, sirow = rows[j] * over, irows[j] * over
            scaled.append((srow, sirow))
            for i in range(j + 1, step):
                ratio = splat[i - j] * over
                rows[i] = rows[i] - splat[i - j] * srow
                irows[i] = irows[i] - splat[i - j] * sirow
                cols[i] = [cols[i][h] - ratio * cols[j][h] for h in range(groups - g)]
            root = lax.rsqrt(pivot)
            upper = jnp.where(sub == j, rows[j] * root, upper)
            lower = jnp.where(sub == j, irows[j] * root, lower)
        factor_ref[base : base + step, :] = jnp.where(lane >= sub + base, upper, 0.0)
        done.append(lower)
        for h in range(g + 1, groups):
            for j in range(step):
                gram[h] = gram[h] - cols[j][h - g] * scaled[j][0]
                inv[h] = inv[h] - cols[j][h - g] * scaled[j][1]
    whole = jnp.concatenate(done, axis=0).T
    high = whole.astype(jnp.bfloat16)
    split_ref[:, :width] = high
    split_ref[:, width:] = (whole - high.astype(jnp.float32)).astype(jnp.bfloat16)


def factor_and_inverse(gram):
    width = gram.shape[0]
    return pl.pallas_call(
        factor_kernel,
        out_shape=[
            jax.ShapeDtypeStruct((width, width), jnp.float32),
            jax.ShapeDtypeStruct((width, 2 * width), jnp.bfloat16),
        ],
        in_specs=[pl.BlockSpec(memory_space=pltpu.VMEM)],
        out_specs=[pl.BlockSpec(memory_space=pltpu.VMEM)] * 2,
        compiler_params=pltpu.CompilerParams(vmem_limit_bytes=32 * 2**20),
        cost_estimate=pl.CostEstimate(flops=0, bytes_accessed=32 * 2**20, transcendentals=0),
    )(gram)


def modes_kernel(which_ref, place_ref, split_ref, *refs):
    out_ref, rows, result, in_sem, out_sem = refs[-5:]
    sources = refs[:-5]
    blocks, cells, width = rows.shape
    for block in range(blocks):
        for index, source in enumerate(sources):

            @pl.when(which_ref[block] == index)
            def _():
                pltpu.make_async_copy(
                    source.at[place_ref[block]], rows.at[block], in_sem.at[block]
                ).start()

    split = split_ref[...]
    group = blocks // 4
    copies = []
    for first in range(0, blocks, group):
        for block in range(first, first + group):
            pltpu.make_async_copy(sources[0].at[0], rows.at[block], in_sem.at[block]).wait()
        for block in range(first, first + group):
            both = jnp.dot(rows[block], split, preferred_element_type=jnp.float32)
            result[pl.ds(block * cells, cells), :] = (both[:, :width] + both[:, width:]).astype(
                jnp.bfloat16
            )
        part = pl.ds(first * cells, group * cells)
        copy = pltpu.make_async_copy(result.at[part], out_ref.at[part], out_sem.at[first])
        copy.start()
        copies.append(copy)
    for copy in copies:
        copy.wait()


def make_modes(which, place, split, sources):
    blocks, cells, width = sources[0].shape
    any_spec = pl.BlockSpec(memory_space=pl.ANY)
    smem = pl.BlockSpec(memory_space=pltpu.SMEM)
    return pl.pallas_call(
        modes_kernel,
        out_shape=jax.ShapeDtypeStruct((blocks * cells, width), jnp.bfloat16),
        in_specs=[smem, smem, pl.BlockSpec(memory_space=pltpu.VMEM)] + [any_spec] * len(sources),
        out_specs=any_spec,
        scratch_shapes=[
            pltpu.VMEM((blocks, cells, width), jnp.bfloat16),
            pltpu.VMEM((blocks * cells, width), jnp.bfloat16),
            pltpu.SemaphoreType.DMA((blocks,)),
            pltpu.SemaphoreType.DMA((blocks,)),
        ],
        compiler_params=pltpu.CompilerParams(vmem_limit_bytes=56 * 2**20),
        cost_estimate=pl.CostEstimate(
            flops=4 * blocks * cells * width * width,
            bytes_accessed=4 * blocks * cells * width,
            transcendentals=0,
        ),
    )(which, place, split, *sources)


def shards(fine, patch_count, block_place):
    slot_total = fine.shape[0]
    blocks = slot_total // 2
    patch_cells = fine.shape[2]
    parity = lax.axis_index("gy") % 2
    held_count = patch_count[0]
    send_half = 1 - parity
    early = blocks // 4
    send_first = send_half * blocks
    sent_a, gram_a = average_range(fine, send_first, held_count, (early,))
    pairs = [(source, source ^ 1) for source in range(lax.axis_size("gy"))]
    moved_a = lax.ppermute(sent_a, "gy", pairs)
    sent_b, kept, gram_b = average_range(
        fine, send_first + early, held_count, (blocks - early, blocks)
    )
    row_total = blocks * patch_cells * lax.axis_size("gx") * lax.axis_size("gy")
    moved_a, gram_b = lax.optimization_barrier((moved_a, gram_b))
    gram = sum_everywhere(gram_a, gram_b, row_total)
    sent_b, gram = lax.optimization_barrier((sent_b, gram))
    moved_b = lax.ppermute(sent_b, "gy", pairs)
    factor, split = factor_and_inverse(gram)

    excess = jnp.where(parity == 0, held_count - blocks, blocks - held_count)
    wanted = block_place[0]
    is_moved = jnp.where(parity == 0, wanted >= blocks + excess, wanted < excess)
    own = jnp.where(parity == 0, wanted, wanted - excess)
    is_sent = own // blocks == send_half
    moved_place = jnp.where(parity == 0, wanted - blocks - excess, wanted)
    place = jnp.clip(jnp.where(is_moved, moved_place, own % blocks), 0, blocks - 1)
    late = (place >= early).astype(jnp.int32)
    which = jnp.where(is_moved, 3 + late, jnp.where(is_sent, 1 + late, 0)).astype(jnp.int32)
    place = jnp.where((which > 0) & (late > 0), place - early, place).astype(jnp.int32)
    modes = make_modes(which, place, split, (kept, sent_a, sent_b, moved_a, moved_b))
    return (factor, modes)


def solution(mesh):
    return jax.shard_map(
        shards,
        mesh=mesh,
        in_specs=(P(("gx", "gy"), None, None, None), P(("gx", "gy")), P(("gx", "gy"), None)),
        out_specs=(P(), P(("gx", "gy"), None)),
        check_vma=False,
    )
```

```python
import functools

import jax
import jax.numpy as jnp
from jax import lax
from jax.experimental import pallas as pl
from jax.experimental.pallas import tpu as pltpu
from jax.sharding import PartitionSpec as P

MESH = pl.DeviceIdType.MESH


def average_kernel(lens, offset, meta_ref, fine_ref, *refs):
    step = pl.program_id(0)
    slots, children, cells, width = fine_ref.shape
    outs, gram_ref, masked = refs[: len(lens)], refs[-2], refs[-1]

    @pl.when(step == 0)
    def _():
        gram_ref[...] = jnp.zeros_like(gram_ref)

    def work(avg_ref):
        piece = 32
        acc = None
        for slot in range(slots):
            number = lax.rem(meta_ref[0] + offset + step * slots + slot, meta_ref[2])
            weight = jnp.where(number < meta_ref[1], 1.0, 0.0).astype(jnp.float32)
            for row in range(0, cells, piece):
                rows = pl.ds(row, piece)
                total = fine_ref[slot, 0, rows, :].astype(jnp.float32)
                for child in range(1, children):
                    total += fine_ref[slot, child, rows, :].astype(jnp.float32)
                mean = total * (1.0 / children)
                avg_ref[slot, rows, :] = mean.astype(jnp.bfloat16)
                masked[slot, rows, :] = (mean * weight).astype(jnp.bfloat16)
            part = masked[slot]
            term = lax.dot_general(
                part, part, (((0,), (0,)), ((), ())), preferred_element_type=jnp.float32
            )
            acc = term if acc is None else acc + term
        gram_ref[...] += acc

    start = 0
    for length, out in zip(lens, outs):
        if len(lens) == 1:
            work(out)
        else:
            pl.when((step >= start) & (step < start + length))(functools.partial(work, out))
        start += length


def average_range(fine, meta, offset, lens):
    slot_total, children, cells, width = fine.shape
    slots = slot_total // 8
    total = sum(lens)
    steps = [length // slots for length in lens]
    starts = [sum(steps[:k]) for k in range(len(steps))]

    def out_spec(start, length):
        return pl.BlockSpec(
            (slots, cells, width), lambda i, meta: (jnp.clip(i - start, 0, length - 1), 0, 0)
        )

    return pl.pallas_call(
        functools.partial(average_kernel, steps, offset),
        grid_spec=pltpu.PrefetchScalarGridSpec(
            num_scalar_prefetch=1,
            grid=(sum(steps),),
            in_specs=[
                pl.BlockSpec(
                    (slots, children, cells, width),
                    lambda i, meta: (lax.rem(meta[0] // slots + offset // slots + i, slot_total // slots), 0, 0, 0),
                )
            ],
            out_specs=[out_spec(start, length) for start, length in zip(starts, steps)]
            + [pl.BlockSpec((width, width), lambda i, meta: (0, 0))],
            scratch_shapes=[pltpu.VMEM((slots, cells, width), jnp.bfloat16)],
        ),
        out_shape=[jax.ShapeDtypeStruct((length, cells, width), jnp.bfloat16) for length in lens]
        + [jax.ShapeDtypeStruct((width, width), jnp.float32)],
        compiler_params=pltpu.CompilerParams(vmem_limit_bytes=56 * 2**20),
        cost_estimate=pl.CostEstimate(
            flops=2 * total * cells * width * width,
            bytes_accessed=4 * total * (children + 1) * cells * width,
            transcendentals=0,
        ),
    )(meta, fine)


def sum_kernel(n_gx, n_gy, row_total, first_ref, second_ref, out_ref, local, parts, planes, send, recv):
    gx, gy = lax.axis_index("gx"), lax.axis_index("gy")
    width = out_ref.shape[0]
    rows = width // n_gx
    barrier = pltpu.get_barrier_semaphore()
    for apart in range(1, n_gx):
        pl.semaphore_signal(
            barrier, inc=1, device_id=(lax.rem(gx + apart, n_gx), gy), device_id_type=MESH
        )
    for apart in range(1, n_gy):
        pl.semaphore_signal(
            barrier, inc=1, device_id=(gx, lax.rem(gy + apart, n_gy)), device_id_type=MESH
        )
    local[...] = first_ref[...] + second_ref[...]
    pl.semaphore_wait(barrier, n_gx + n_gy - 2)

    copies = []
    for apart in range(1, n_gx):
        there = lax.rem(gx + apart, n_gx)
        copy = pltpu.make_async_remote_copy(
            src_ref=local.at[pl.ds(pl.multiple_of(there * rows, rows), rows)],
            dst_ref=parts.at[apart],
            send_sem=send.at[0, apart],
            recv_sem=recv.at[0, apart],
            device_id=(there, gy),
            device_id_type=MESH,
        )
        copy.start()
        copies.append(copy)
    total = local[pl.ds(pl.multiple_of(gx * rows, rows), rows), :]
    for apart in range(1, n_gx):
        copies[apart - 1].wait_recv()
        total += parts[apart]
    planes[gy] = total

    for apart in range(1, n_gy):
        copy = pltpu.make_async_remote_copy(
            src_ref=planes.at[gy],
            dst_ref=planes.at[gy],
            send_sem=send.at[1, apart],
            recv_sem=recv.at[1, apart],
            device_id=(gx, lax.rem(gy + apart, n_gy)),
            device_id_type=MESH,
        )
        copy.start()
        copies.append(copy)
    for apart in range(1, n_gy):
        copies[n_gx - 2 + apart].wait_recv()
    total = planes[0]
    for plane in range(1, n_gy):
        total += planes[plane]
    mine = pl.ds(pl.multiple_of(gx * rows, rows), rows)
    out_ref[mine, :] = total / row_total

    last = []
    for apart in range(1, n_gx):
        copy = pltpu.make_async_remote_copy(
            src_ref=out_ref.at[mine],
            dst_ref=out_ref.at[mine],
            send_sem=send.at[2, apart],
            recv_sem=recv.at[2, apart],
            device_id=(lax.rem(gx + apart, n_gx), gy),
            device_id_type=MESH,
        )
        copy.start()
        last.append(copy)
    for copy in copies:
        copy.wait_send()
    for copy in last:
        copy.wait()


def sum_everywhere(first, second, row_total):
    n_gx, n_gy = lax.axis_size("gx"), lax.axis_size("gy")
    width = first.shape[0]
    rows = width // n_gx
    most = max(n_gx, n_gy)
    return pl.pallas_call(
        functools.partial(sum_kernel, n_gx, n_gy, row_total),
        out_shape=jax.ShapeDtypeStruct((width, width), jnp.float32),
        in_specs=[pl.BlockSpec(memory_space=pltpu.VMEM)] * 2,
        out_specs=pl.BlockSpec(memory_space=pltpu.VMEM),
        scratch_shapes=[
            pltpu.VMEM((width, width), jnp.float32),
            pltpu.VMEM((n_gx, rows, width), jnp.float32),
            pltpu.VMEM((n_gy, rows, width), jnp.float32),
            pltpu.SemaphoreType.DMA((3, most)),
            pltpu.SemaphoreType.DMA((3, most)),
        ],
        compiler_params=pltpu.CompilerParams(collective_id=0, has_side_effects=True),
        cost_estimate=pl.CostEstimate(flops=0, bytes_accessed=2**18, transcendentals=0),
    )(first, second)


def factor_kernel(gram_ref, factor_ref, split_ref):
    width = gram_ref.shape[0]
    step = 8
    groups = width // step
    lane = lax.broadcasted_iota(jnp.int32, (step, width), 1)
    sub = lax.broadcasted_iota(jnp.int32, (step, width), 0)
    gram = [gram_ref[g * step : (g + 1) * step, :] for g in range(groups)]
    inv = [(lane == sub + g * step).astype(jnp.float32) for g in range(groups)]
    done = []
    for g in range(groups):
        base = g * step
        cols = [
            [jnp.broadcast_to(gram[h][:, base + j : base + j + 1], (step, width)) for h in range(g, groups)]
            for j in range(step)
        ]
        rows = [jnp.broadcast_to(gram[g][j : j + 1, :], (step, width)) for j in range(step)]
        irows = [jnp.broadcast_to(inv[g][j : j + 1, :], (step, width)) for j in range(step)]
        scaled = []
        upper = jnp.zeros((step, width), jnp.float32)
        lower = jnp.zeros((step, width), jnp.float32)
        for j in range(step):
            splat = [jnp.broadcast_to(cols[j][0][i : i + 1, :], (step, width)) for i in range(j, step)]
            pivot = splat[0]
            over = 1.0 / pivot
            srow, sirow = rows[j] * over, irows[j] * over
            scaled.append((srow, sirow))
            for i in range(j + 1, step):
                ratio = splat[i - j] * over
                rows[i] = rows[i] - splat[i - j] * srow
                irows[i] = irows[i] - splat[i - j] * sirow
                cols[i] = [cols[i][h] - ratio * cols[j][h] for h in range(groups - g)]
            root = lax.rsqrt(pivot)
            upper = jnp.where(sub == j, rows[j] * root, upper)
            lower = jnp.where(sub == j, irows[j] * root, lower)
        factor_ref[base : base + step, :] = jnp.where(lane >= sub + base, upper, 0.0)
        done.append(lower)
        for h in range(g + 1, groups):
            for j in range(step):
                gram[h] = gram[h] - cols[j][h - g] * scaled[j][0]
                inv[h] = inv[h] - cols[j][h - g] * scaled[j][1]
    whole = jnp.concatenate(done, axis=0).T
    high = whole.astype(jnp.bfloat16)
    split_ref[:, :width] = high
    split_ref[:, width:] = (whole - high.astype(jnp.float32)).astype(jnp.bfloat16)


def factor_and_inverse(gram):
    width = gram.shape[0]
    return pl.pallas_call(
        factor_kernel,
        out_shape=[
            jax.ShapeDtypeStruct((width, width), jnp.float32),
            jax.ShapeDtypeStruct((width, 2 * width), jnp.bfloat16),
        ],
        in_specs=[pl.BlockSpec(memory_space=pltpu.VMEM)],
        out_specs=[pl.BlockSpec(memory_space=pltpu.VMEM)] * 2,
        compiler_params=pltpu.CompilerParams(vmem_limit_bytes=32 * 2**20),
        cost_estimate=pl.CostEstimate(flops=0, bytes_accessed=32 * 2**20, transcendentals=0),
    )(gram)


def modes_kernel(which_ref, place_ref, split_ref, *refs):
    out_ref, rows, result, in_sem, out_sem = refs[-5:]
    sources = refs[:-5]
    blocks, cells, width = rows.shape
    for block in range(blocks):
        for index, source in enumerate(sources):

            @pl.when(which_ref[block] == index)
            def _():
                pltpu.make_async_copy(
                    source.at[place_ref[block]], rows.at[block], in_sem.at[block]
                ).start()

    split = split_ref[...]
    group = blocks // 4
    copies = []
    for first in range(0, blocks, group):
        for block in range(first, first + group):
            pltpu.make_async_copy(sources[0].at[0], rows.at[block], in_sem.at[block]).wait()
        for block in range(first, first + group):
            both = jnp.dot(rows[block], split, preferred_element_type=jnp.float32)
            result[pl.ds(block * cells, cells), :] = (both[:, :width] + both[:, width:]).astype(
                jnp.bfloat16
            )
        part = pl.ds(first * cells, group * cells)
        copy = pltpu.make_async_copy(result.at[part], out_ref.at[part], out_sem.at[first])
        copy.start()
        copies.append(copy)
    for copy in copies:
        copy.wait()


def make_modes(which, place, split, sources):
    blocks, cells, width = sources[0].shape
    any_spec = pl.BlockSpec(memory_space=pl.ANY)
    smem = pl.BlockSpec(memory_space=pltpu.SMEM)
    return pl.pallas_call(
        modes_kernel,
        out_shape=jax.ShapeDtypeStruct((blocks * cells, width), jnp.bfloat16),
        in_specs=[smem, smem, pl.BlockSpec(memory_space=pltpu.VMEM)] + [any_spec] * len(sources),
        out_specs=any_spec,
        scratch_shapes=[
            pltpu.VMEM((blocks, cells, width), jnp.bfloat16),
            pltpu.VMEM((blocks * cells, width), jnp.bfloat16),
            pltpu.SemaphoreType.DMA((blocks,)),
            pltpu.SemaphoreType.DMA((blocks,)),
        ],
        compiler_params=pltpu.CompilerParams(vmem_limit_bytes=56 * 2**20),
        cost_estimate=pl.CostEstimate(
            flops=4 * blocks * cells * width * width,
            bytes_accessed=4 * blocks * cells * width,
            transcendentals=0,
        ),
    )(which, place, split, *sources)


def shards(fine, patch_count, block_place):
    slot_total = fine.shape[0]
    blocks = slot_total // 2
    patch_cells = fine.shape[2]
    parity = lax.axis_index("gy") % 2
    held_count = patch_count[0]
    send_half = 1 - parity
    early = 3 * blocks // 4
    send_first = send_half * blocks
    meta = jnp.stack([send_first, held_count, jnp.int32(slot_total)])
    sent_a, gram_a = average_range(fine, meta, 0, (early,))
    pairs = [(source, source ^ 1) for source in range(lax.axis_size("gy"))]
    moved_a = lax.ppermute(sent_a, "gy", pairs)
    sent_b, kept, gram_b = average_range(fine, meta, early, (blocks - early, blocks))
    row_total = blocks * patch_cells * lax.axis_size("gx") * lax.axis_size("gy")
    gram = sum_everywhere(gram_a, gram_b, row_total)
    sent_b, gram, moved_a = lax.optimization_barrier((sent_b, gram, moved_a))
    moved_b = lax.ppermute(sent_b, "gy", pairs)
    factor, split = factor_and_inverse(gram)

    excess = jnp.where(parity == 0, held_count - blocks, blocks - held_count)
    wanted = block_place[0]
    is_moved = jnp.where(parity == 0, wanted >= blocks + excess, wanted < excess)
    own = jnp.where(parity == 0, wanted, wanted - excess)
    is_sent = own // blocks == send_half
    moved_place = jnp.where(parity == 0, wanted - blocks - excess, wanted)
    place = jnp.clip(jnp.where(is_moved, moved_place, own % blocks), 0, blocks - 1)
    late = (place >= early).astype(jnp.int32)
    which = jnp.where(is_moved, 3 + late, jnp.where(is_sent, 1 + late, 0)).astype(jnp.int32)
    place = jnp.where((which > 0) & (late > 0), place - early, place).astype(jnp.int32)
    modes = make_modes(which, place, split, (kept, sent_a, sent_b, moved_a, moved_b))
    return (factor, modes)


def solution(mesh):
    return jax.shard_map(
        shards,
        mesh=mesh,
        in_specs=(P(("gx", "gy"), None, None, None), P(("gx", "gy")), P(("gx", "gy"), None)),
        out_specs=(P(), P(("gx", "gy"), None)),
        check_vma=False,
    )
```
